128 devices in a mesh: grp: 4 (over y), mem: 32 (over x, z, core).
Axes of the slice: x: 4, y: 4, z: 4, core: 2. Of those that a mesh axis runs over, the one named last changes fastest.
Arguments:
- weights: bfloat16 [64, 1536, 4096], P('mem', None, 'grp'), may hold values from -0.09375 to 0.09375
- stored_order: int32 [64], replicated, may hold values from 0 to 63, each once
- assignment: int32 [64, 1], replicated, may hold values from 0 to 3; in each aligned block of 64 rows (0 to 63, 64 to 127, ...) at most 24 rows name the same one
- init_basis: bfloat16 [4, 4096, 512], P('grp'), may hold values from -6 to 6
Outputs:
- basis: bfloat16 [4, 4096, 512], P('grp', 'mem')
- coefficients: bfloat16 [4, 24, 1536, 512], P('grp', None, 'mem')
The draws below stay inside these ranges and needn't reach their ends.
Inputs may be any that keep to these rules, and one draw needn't show every extreme that they name: `stored_order`: each expert id appears exactly once. `assignment`: every group has at least one expert and at most 24; some group has exactly 24.
All inputs are finite; a program needn't handle non-finite values.
Results may differ from the reference program's by a relative error of at most 0.024.
Values may be sent and summed in bfloat16 or wider, within the bound.
A program may use at most 192 MiB of HBM per device.

```python
import math
import jax
import jax.numpy as jnp
import numpy as np
from jax import lax

D = 4096
F = 1536
EXPERTS = 64
RANK = 512
ITERS = 2
NS_STEPS = 6
GROUPS = 4
CAP = 24
N_MEM = 32


def steps_of(own_key, dims, cuts, least, top_value):
    def one(axis_at, parts):
        steps = jax.random.uniform(jax.random.fold_in(jax.random.fold_in(own_key, 6), axis_at), (parts,), jnp.float32, least / len(cuts), top_value / len(cuts))
        return jnp.repeat(jnp.exp(steps), dims[axis_at] // parts).reshape((-1,) + (1,) * (len(dims) - axis_at - 1))

    gain = one(*cuts[0])
    for cut in cuts[1:]:
        gain = gain * one(*cut)
    return gain


def deal_out(stream_key, own, number, rows, amount, top, limit, lean):
    order = jax.random.permutation(stream_key, amount)
    heavy_load, common = portions_of(amount, rows * top, limit, lean, True), portions_of(amount, rows * top, limit, lean, False)
    places = jnp.arange(amount)

    def named(lengths, turn):
        used = int((lengths > 0).sum())
        fixed = max(1, used // 4)
        passed = fixed + (places - fixed + turn * (used - fixed)) % max(1, amount - fixed)
        return jnp.zeros((amount,), jnp.int32).at[order[jnp.where(places < fixed, places, passed)]].set(jnp.asarray(lengths, jnp.int32))

    lengths = jnp.where(number % 4 == 0, named(heavy_load, number // 4), named(common, number - number // 4 - 1))
    mixed = jax.random.permutation(jax.random.fold_in(own, 3), amount)
    giver, sink = mixed[0:amount // 2 * 2:2], mixed[1:amount // 2 * 2:2]
    margin = jnp.minimum(lengths[giver] - 1, limit - lengths[sink]) // 2
    margin = jnp.where((giver == order[0]) | (sink == order[0]) | (lengths[sink] == 0), 0, jnp.maximum(margin, 0))
    passed = jax.random.randint(jax.random.fold_in(own, 4), (amount // 2,), 0, 1 << 20) % (margin + 1)
    lengths = lengths.at[giver].add(-passed).at[sink].add(passed)
    labels = jnp.searchsorted(jnp.cumsum(lengths), jnp.arange(rows * top), side="right").astype(jnp.int32)
    listing = labels.reshape(top, rows).T
    listing = listing[jax.random.permutation(jax.random.fold_in(own, 1), rows)]
    turn = jax.random.randint(jax.random.fold_in(own, 2), (rows, 1), 0, top)
    return jnp.take_along_axis(listing, (jnp.arange(top)[None, :] + turn) % top, axis=1)


def portions_of(number_of, total, limit, slope, full):
    weights = [(1 << 20) // math.isqrt(standing ** slope) + 1 for standing in range(1, number_of + 1)]
    largest = limit if full else min(limit, max(-(-total // number_of), total * weights[0] // sum(weights)))
    least = 1 if total - largest >= number_of - 1 else 0
    holding, surplus = [largest] + [least] * (number_of - 1), total - largest - least * (number_of - 1)
    while surplus > 0:
        candidates = [i for i in range(1, number_of) if holding[i] < largest] or [i for i in range(1, number_of) if holding[i] < limit]
        whole, left = sum([weights[i] for i in candidates]), surplus
        for i in candidates:
            more = min(limit - holding[i], max(1, left * weights[i] // whole), surplus)
            holding[i] = holding[i] + more
            surplus = surplus - more
    return np.array(holding)


def normal_values(rng, extent, width, limit, cuts=(), kind=jnp.bfloat16):
    array = width * jax.random.normal(rng, extent, jnp.float32)
    if cuts:
        array = array * steps_of(rng, extent, cuts, -0.22, 0.18)
    return jnp.clip(array, -limit, limit).astype(kind)


def setup_inputs(seed: int = 0) -> dict:
    key_of = jax.random.split(jax.random.key(seed), 5)
    weights = normal_values(key_of[0], (EXPERTS, F, D), D ** -0.5, 0.09375, ((0, 32), (2, 4)))
    stored_order = jax.random.permutation(key_of[1], EXPERTS).astype(jnp.int32)
    assignment_keys = jax.random.split(jax.random.fold_in(key_of[2], 1), EXPERTS // EXPERTS)
    assignment_turns = jax.random.permutation(jax.random.fold_in(key_of[2], 3), EXPERTS // EXPERTS)
    assignment = jax.vmap(lambda own, number: deal_out(jax.random.fold_in(key_of[2], 2), own, number, EXPERTS, GROUPS, 1, CAP, 1))(assignment_keys, assignment_turns).reshape((EXPERTS, 1))
    init_basis = normal_values(key_of[3], (GROUPS, D, RANK), 1.0, 6.0, ((0, 4),))
    return dict(weights=weights, stored_order=stored_order, assignment=assignment, init_basis=init_basis)


def slot_positions(stored_order, assignment, group_id):
    assign = assignment[:, 0]
    member = (assign == group_id).astype(jnp.int32)
    ranking = jnp.cumsum(member) - member
    slot_hit = (member[None, :] == 1) & (ranking[None, :] == jnp.arange(CAP, dtype=jnp.int32)[:, None])
    holder = (stored_order[None, :] == jnp.arange(EXPERTS, dtype=jnp.int32)[:, None]).astype(jnp.int32)
    picker = jnp.dot(slot_hit.astype(jnp.int32), holder)
    positions = lax.optimization_barrier(jnp.sum(picker * jnp.arange(EXPERTS, dtype=jnp.int32)[None, :], axis=1)).astype(jnp.int32)
    filled = lax.optimization_barrier(jnp.sum(picker, axis=1))
    return (positions, filled)

def one_group(weights, stored_order, assignment, group_id, start_basis):
    positions, filled = slot_positions(stored_order, assignment, group_id)
    regrouped = jnp.take(weights, positions, axis=0) * filled[:, None, None].astype(jnp.bfloat16)
    wide = regrouped.astype(jnp.float32)
    current = start_basis
    identity = jnp.eye(RANK, dtype=jnp.float32)
    for sweep in range(ITERS):
        projected = jnp.einsum('kfd,dr->kfr', wide, current.astype(jnp.float32), precision=lax.Precision.HIGHEST).astype(jnp.bfloat16)
        blocks = wide.reshape(CAP, N_MEM, F // N_MEM, D)
        pieces = projected.astype(jnp.float32).reshape(CAP, N_MEM, F // N_MEM, RANK)
        partial_value = jnp.einsum('kbcd,kbcr->bdr', blocks, pieces, precision=lax.Precision.HIGHEST).astype(jnp.bfloat16)
        image = lax.optimization_barrier(jnp.sum(partial_value.astype(jnp.float32), axis=0))
        gram = jnp.dot(image.T, image, precision=lax.Precision.HIGHEST)
        frob = jnp.sqrt(jnp.sum(gram * gram)) + 1e-06
        scaled = gram / frob
        root = identity
        for inner in range(NS_STEPS):
            factor = 1.5 * identity - 0.5 * jnp.dot(root, scaled, precision=lax.Precision.HIGHEST)
            scaled = jnp.dot(scaled, factor, precision=lax.Precision.HIGHEST)
            root = jnp.dot(factor, root, precision=lax.Precision.HIGHEST)
        current = (jnp.dot(image, root, precision=lax.Precision.HIGHEST) * jnp.sqrt(D / frob)).astype(jnp.bfloat16)
    coefficients = jnp.einsum('kfd,dr->kfr', wide, current.astype(jnp.float32), precision=lax.Precision.HIGHEST).astype(jnp.bfloat16)
    return (current, coefficients)

def reference(weights, stored_order, assignment, init_basis):

    def handle(items):
        return one_group(weights, stored_order, assignment, items[0], items[1])
    basis, coefficients = lax.map(handle, (jnp.arange(GROUPS, dtype=jnp.int32), init_basis))
    return (basis, coefficients)
```

```python
import jax
import jax.numpy as jnp
from jax import lax
from jax.experimental import pallas as pl
from jax.experimental.pallas import tpu as pltpu
from jax.sharding import PartitionSpec as P

ITERS = 2
NS_STEPS = 6
MESH = pl.DeviceIdType.MESH
F32 = jnp.float32
BF16 = jnp.bfloat16
ROW = 16
VMEM_LIMIT = 60 * 1024 * 1024


def remote(src, dst, send, recv, device):
    return pltpu.make_async_remote_copy(
        src_ref=src, dst_ref=dst, send_sem=send, recv_sem=recv, device_id=device, device_id_type=MESH
    )


def greet(peers):
    barrier = pltpu.get_barrier_semaphore()
    for peer in peers:
        pl.semaphore_signal(barrier, inc=1, device_id=peer, device_id_type=MESH)
    pl.semaphore_wait(barrier, len(peers))


def slot_sources(stored_order, assignment, groups, capacity):
    assign = assignment[:, 0]
    experts = assign.shape[0]
    ids = jnp.arange(experts, dtype=jnp.int32)
    same = (assign[None, :] == assign[:, None]) & (ids[None, :] < ids[:, None])
    slot = assign * capacity + jnp.sum(same.astype(jnp.int32), axis=1)
    held = (stored_order[:, None] == ids[None, :]).astype(jnp.int32)
    slot_of_position = jnp.sum(held * slot[None, :], axis=1)
    slots = jnp.arange(groups * capacity, dtype=jnp.int32)
    hit = (slot_of_position[None, :] == slots[:, None]).astype(jnp.int32)
    return experts + jnp.sum(hit * (ids - experts)[None, :], axis=1)


def regroup(weights, sources, groups, members, capacity):
    held, rows, columns = weights.shape
    experts = held * members
    share = rows // members
    row_parts, col_parts = share // ROW, 2
    width = columns // col_parts
    chunks = [(r, h) for r in range(row_parts) for h in range(col_parts)]
    total = len(chunks)

    def kernel(sources_ref, w_ref, out_ref, packed, own_sem, a_send, a_recv, b_send, b_recv, *landed):
        g, m = lax.axis_index("grp"), lax.axis_index("mem")
        others = [(g, m ^ (k ^ (k >> 1))) for k in range(1, members)]
        across = [(lax.rem(g + k, groups), m) for k in range(1, groups)]
        greet(others + across)

        def piece(ci, member):
            r, h = chunks[ci]
            return w_ref.at[:, pl.ds(share * member + ROW * r, ROW), pl.ds(width * h, width)]

        def own(ci):
            return pltpu.make_async_copy(
                piece(ci, m), landed[ci].at[pl.ds(held * m, held)], own_sem.at[ci]
            )

        for ci in range(total):
            own(ci).start()
            for dev in others:
                remote(
                    piece(ci, dev[1]), landed[ci].at[pl.ds(held * m, held)], a_send.at[ci], a_recv.at[ci], dev
                ).start()
            landed[ci][experts] = jnp.zeros((ROW, width), BF16)

        def target(ci, source_group):
            r, h = chunks[ci]
            return out_ref.at[r, :, pl.ds(columns * source_group + width * h, width)]

        def keep(ci):
            return pltpu.make_async_copy(packed.at[ci, g], target(ci, g), own_sem.at[total + ci])

        def cross(ci, k):
            dev = across[k - 1]
            return remote(packed.at[ci, dev[0]], target(ci, g), b_send.at[ci, k], b_recv.at[ci, k], dev)

        for ci in range(total):
            own(ci).wait()
            arrivals = landed[ci].at[pl.ds(0, experts - held)]
            pltpu.make_async_copy(arrivals, arrivals, a_recv.at[ci]).wait()

            def pack(k, carry, ci=ci):
                for group in range(groups):
                    packed[ci, group, pl.ds(pl.multiple_of(k * ROW, ROW), ROW), :] = landed[ci][
                        sources_ref[group * capacity + k]
                    ]
                return carry

            lax.fori_loop(0, capacity, pack, 0)
            for k in range(1, groups):
                cross(ci, k).start()
            keep(ci).start()
        for ci in range(total):
            keep(ci).wait()
            for k in range(1, groups):
                cross(ci, k).wait()
            sent = landed[ci].at[pl.ds(0, experts - held)]
            pltpu.make_async_copy(sent, sent, a_send.at[ci]).wait()

    return pl.pallas_call(
        kernel,
        out_shape=jax.ShapeDtypeStruct((row_parts, capacity * ROW, groups * columns), BF16),
        in_specs=[pl.BlockSpec(memory_space=pltpu.SMEM), pl.BlockSpec(memory_space=pl.ANY)],
        out_specs=pl.BlockSpec(memory_space=pl.ANY),
        scratch_shapes=[
            pltpu.VMEM((total, groups, capacity * ROW, width), BF16),
            pltpu.SemaphoreType.DMA((2 * total,)),
            pltpu.SemaphoreType.DMA((total,)),
            pltpu.SemaphoreType.DMA((total,)),
            pltpu.SemaphoreType.DMA((total, groups)),
            pltpu.SemaphoreType.DMA((total, groups)),
        ]
        + [pltpu.VMEM((experts + 1, ROW, width), BF16)] * total,
        compiler_params=pltpu.CompilerParams(
            collective_id=0, has_side_effects=True, vmem_limit_bytes=VMEM_LIMIT
        ),
        cost_estimate=pl.CostEstimate(flops=0, bytes_accessed=32 << 20, transcendentals=0),
        name="regroup",
    )(sources, weights)


NN = (((1,), (0,)), ((), ()))
NT = (((1,), (1,)), ((), ()))


def mm(a, b, dims=NN):
    return lax.dot_general(a, b, dims, preferred_element_type=F32)


def split(x):
    high = x.astype(BF16)
    return high, (x - high.astype(F32)).astype(BF16)


def mm3(a, b, dims=NN):
    return mm(a[0], b[0], dims) + (mm(a[0], b[1], dims) + mm(a[1], b[0], dims))


def eye(n):
    return (lax.broadcasted_iota(jnp.int32, (n, n), 0) == lax.broadcasted_iota(jnp.int32, (n, n), 1)).astype(F32)


def iterate(regrouped, start, capacity):
    parts, part_rows, depth = regrouped.shape
    rank = start.shape[1]
    rows = parts * part_rows
    chunk = depth // 8
    half = rank // 2
    quarter = half // 4

    def kernel(
        w_ref, b_ref, basis_ref, coef_ref,
        proj, proj_t, full, out1, in1, sum1, in2, sum2, in3, root_hi, root_lo, scale_ref,
        send, recv,
    ):
        g, m = lax.axis_index("grp"), lax.axis_index("mem")
        x, z, c = m // 8, lax.rem(m // 2, 4), lax.rem(m, 2)
        sib = 1 - c
        member = lambda xx, zz, cc: (g, 8 * xx + 2 * zz + cc)
        turn = lambda v, o: lax.rem(v + o, 4)
        sibling = member(x, z, sib)
        xs = [None] + [member(turn(x, o), z, c) for o in (1, 2, 3)]
        zs = [None] + [member(x, turn(z, o), c) for o in (1, 2, 3)]
        first, second = (xs, zs), (zs, xs)
        place, other = (x, z), (z, x)
        greet([sibling] + xs[1:] + zs[1:])

        def copy(stage, h, o, src, dst, dev):
            return remote(src, dst, send.at[stage, h, o], recv.at[stage, h, o], dev)

        HALVES = (0, 1)
        steps = [(o, h) for o in (1, 2, 3, 0) for h in HALVES]

        for r in range(parts):
            proj[r * part_rows : (r + 1) * part_rows, :] = mm(w_ref[r], b_ref[...])
        root_hi[...] = eye(rank).astype(BF16)
        root_lo[...] = jnp.zeros((rank, rank), BF16)
        scale_ref[0] = jnp.float32(1.0)

        def columns_of(which):
            return pl.ds(pl.multiple_of(which * chunk, chunk), chunk)

        def image_piece(core, q, h):
            total = None
            for r in range(parts):
                term = mm(
                    proj_t[h * half : (h + 1) * half, r * part_rows : (r + 1) * part_rows],
                    w_ref[r, :, columns_of(core * 4 + q)],
                )
                total = term if total is None else total + term
            return total

        def sweep(it, carry):
            root = (root_hi[...], root_lo[...])
            for r in range(parts):
                at = slice(r * part_rows, (r + 1) * part_rows)
                proj_t[:, at] = (mm3(root, split(proj[at, :]), NT) * scale_ref[0]).astype(BF16)

            ship1 = {}
            for o, h in steps:
                out1[h, o] = image_piece(sib, turn(place[h], o), h).astype(BF16)
                ship1[o, h] = copy(0, h, o, out1.at[h, o], in1.at[h, o], sibling)
                ship1[o, h].start()
            ship2 = {}
            for o, h in steps:
                mine = image_piece(c, turn(place[h], o), h)
                ship1[o, h].wait_recv()
                sum1[h, o] = (mine + in1[h, o].astype(F32)).astype(BF16)
                if o:
                    ship2[o, h] = copy(1, h, o, sum1.at[h, o], in2.at[h, o], first[h][o])
                    ship2[o, h].start()
            ship3 = {}
            for h in HALVES:
                for o in (1, 2, 3):
                    ship2[o, h].wait_recv()
                sum2[h] = (
                    (sum1[h, 0].astype(F32) + in2[h, 1].astype(F32))
                    + (in2[h, 2].astype(F32) + in2[h, 3].astype(F32))
                ).astype(BF16)
                for o in (1, 2, 3):
                    rows_there = pl.ds(pl.multiple_of(turn(other[h], o) * quarter, quarter), quarter)
                    ship3[o, h] = copy(2, h, o, sum2.at[h, rows_there], in3.at[h, o], second[h][o])
                    ship3[o, h].start()
            ship4, ship5, ship6 = {}, {}, {}
            for h in HALVES:
                for o in (1, 2, 3):
                    ship3[o, h].wait_recv()
                mine_rows = pl.ds(pl.multiple_of(other[h] * quarter, quarter), quarter)
                here = pl.ds(pl.multiple_of(h * half + other[h] * quarter, quarter), quarter)
                total = (sum2[h, mine_rows].astype(F32) + in3[h, 1].astype(F32)) + (
                    in3[h, 2].astype(F32) + in3[h, 3].astype(F32)
                )
                spot = full.at[c * 4 + place[h], here]
                full[c * 4 + place[h], here, :] = total.astype(BF16)
                for o in (1, 2, 3):
                    ship4[o, h] = copy(3, h, o, spot, spot, second[h][o])
                    ship4[o, h].start()

            def spot_of(core, q, h):
                return full.at[core * 4 + q, pl.ds(h * half, half)]

            def absorb(core, q, h, start):
                cols = slice(h * half, (h + 1) * half)
                block = full[core * 4 + q, h * half : (h + 1) * half, :]
                for r in range(parts):
                    at = slice(r * part_rows, (r + 1) * part_rows)
                    term = mm(w_ref[r, :, columns_of(core * 4 + q)], block, NT)
                    if start:
                        proj[at, cols] = term
                    else:
                        proj[at, cols] += term

            for h in HALVES:
                for o in (1, 2, 3):
                    ship4[o, h].wait_recv()
                spot = spot_of(c, place[h], h)
                for o in (1, 2, 3):
                    ship5[o, h] = copy(4, h, o, spot, spot, first[h][o])
                    ship5[o, h].start()
                ship6[0, h] = copy(5, h, 0, spot, spot, sibling)
                ship6[0, h].start()
            for h in HALVES:
                absorb(c, place[h], h, True)
            for h in HALVES:
                ship6[0, h].wait_recv()
                absorb(sib, place[h], h, False)
            for o in (1, 3, 2):
                for h in HALVES:
                    q = turn(place[h], 4 - o)
                    ship5[o, h].wait_recv()
                    spot = spot_of(c, q, h)
                    ship6[o, h] = copy(5, h, o, spot, spot, sibling)
                    ship6[o, h].start()
                for h in HALVES:
                    absorb(c, turn(place[h], 4 - o), h, False)
                for h in HALVES:
                    ship6[o, h].wait_recv()
                    absorb(sib, turn(place[h], 4 - o), h, False)

            gram = None
            for d in range(8):
                term = mm(full[d], full[d], NT)
                gram = term if gram is None else gram + term
            frob = jnp.sqrt(jnp.sum(gram * gram)) + 1e-06
            scaled = split(gram / frob)
            ident = eye(rank)
            factor = split(1.5 * ident - 0.5 * (scaled[0].astype(F32) + scaled[1].astype(F32)))
            root = factor
            for inner in range(1, NS_STEPS):
                scaled = split(mm3(scaled, factor))
                factor = split(1.5 * ident - 0.5 * mm3(root, scaled))
                root = split(mm3(factor, root))
            root_hi[...] = root[0]
            root_lo[...] = root[1]
            scale_ref[0] = jnp.sqrt(jnp.float32(depth) / frob)

            for o, h in steps:
                ship1[o, h].wait_send()
                ship6[o, h].wait_send()
                if o:
                    for ship in (ship2, ship3, ship4, ship5):
                        ship[o, h].wait_send()
            return carry

        lax.fori_loop(0, ITERS, sweep, 0)

        root = (root_hi[...], root_lo[...])
        scale = scale_ref[0]
        for r in range(parts):
            value = mm3(split(proj[r * part_rows : (r + 1) * part_rows, :]), root) * scale
            coef_ref[:, r * ROW : (r + 1) * ROW, :] = value.astype(BF16).reshape(capacity, ROW, rank)
        block = full[m // 4, :, pl.ds(pl.multiple_of(lax.rem(m, 4) * 128, 128), 128)]
        turned = mm(eye(128).astype(BF16), block, NT).astype(BF16)
        basis_ref[...] = ((mm(turned, root[0]) + mm(turned, root[1])) * scale).astype(BF16)

    return pl.pallas_call(
        kernel,
        out_shape=(
            jax.ShapeDtypeStruct((128, rank), BF16),
            jax.ShapeDtypeStruct((capacity, parts * ROW, rank), BF16),
        ),
        in_specs=[pl.BlockSpec(memory_space=pltpu.VMEM)] * 2,
        out_specs=(pl.BlockSpec(memory_space=pltpu.VMEM),) * 2,
        scratch_shapes=[
            pltpu.VMEM((rows, rank), F32),
            pltpu.VMEM((rank, rows), BF16),
            pltpu.VMEM((8, rank, chunk), BF16),
            pltpu.VMEM((2, 4, half, chunk), BF16),
            pltpu.VMEM((2, 4, half, chunk), BF16),
            pltpu.VMEM((2, 4, half, chunk), BF16),
            pltpu.VMEM((2, 4, half, chunk), BF16),
            pltpu.VMEM((2, half, chunk), BF16),
            pltpu.VMEM((2, 4, quarter, chunk), BF16),
            pltpu.VMEM((rank, rank), BF16),
            pltpu.VMEM((rank, rank), BF16),
            pltpu.SMEM((1,), F32),
            pltpu.SemaphoreType.DMA((6, 2, 4)),
            pltpu.SemaphoreType.DMA((6, 2, 4)),
        ],
        compiler_params=pltpu.CompilerParams(
            collective_id=1, has_side_effects=True, vmem_limit_bytes=VMEM_LIMIT
        ),
        cost_estimate=pl.CostEstimate(flops=40 << 30, bytes_accessed=32 << 20, transcendentals=0),
        name="iterate",
    )(regrouped, start)


def body(weights, stored_order, assignment, init_basis):
    groups, members = lax.axis_size("grp"), lax.axis_size("mem")
    experts = weights.shape[0] * members
    capacity = experts // groups + experts // (2 * groups)
    sources = slot_sources(stored_order, assignment, groups, capacity)
    regrouped = regroup(weights, sources, groups, members, capacity)
    basis, coefficients = iterate(regrouped, init_basis[0], capacity)
    return (basis[None], coefficients[None])


def solution(mesh):
    return jax.shard_map(
        body,
        mesh=mesh,
        in_specs=(P("mem", None, "grp"), P(), P(), P("grp", None, None)),
        out_specs=(P("grp", "mem", None), P("grp", None, "mem", None)),
        check_vma=False,
    )
```

```python
import jax
import jax.numpy as jnp
from jax import lax
from jax.experimental import pallas as pl
from jax.experimental.pallas import tpu as pltpu
from jax.sharding import PartitionSpec as P

ITERS = 2
NS_STEPS = 6
MESH = pl.DeviceIdType.MESH
F32 = jnp.float32
BF16 = jnp.bfloat16
ROW = 16
VMEM_LIMIT = 60 * 1024 * 1024


def remote(src, dst, send, recv, device):
    return pltpu.make_async_remote_copy(
        src_ref=src, dst_ref=dst, send_sem=send, recv_sem=recv, device_id=device, device_id_type=MESH
    )


def greet(peers):
    barrier = pltpu.get_barrier_semaphore()
    for peer in peers:
        pl.semaphore_signal(barrier, inc=1, device_id=peer, device_id_type=MESH)
    pl.semaphore_wait(barrier, len(peers))


def slot_sources(stored_order, assignment, groups, capacity):
    assign = assignment[:, 0]
    experts = assign.shape[0]
    ids = jnp.arange(experts, dtype=jnp.int32)
    same = (assign[None, :] == assign[:, None]) & (ids[None, :] < ids[:, None])
    slot = assign * capacity + jnp.sum(same.astype(jnp.int32), axis=1)
    held = (stored_order[:, None] == ids[None, :]).astype(jnp.int32)
    slot_of_position = jnp.sum(held * slot[None, :], axis=1)
    slots = jnp.arange(groups * capacity, dtype=jnp.int32)
    hit = (slot_of_position[None, :] == slots[:, None]).astype(jnp.int32)
    return experts + jnp.sum(hit * (ids - experts)[None, :], axis=1)


NN = (((1,), (0,)), ((), ()))
NT = (((1,), (1,)), ((), ()))


def mm(a, b, dims=NN):
    return lax.dot_general(a, b, dims, preferred_element_type=F32)


def split(x):
    high = x.astype(BF16)
    return high, (x - high.astype(F32)).astype(BF16)


def mm3(a, b, dims=NN):
    return mm(a[0], b[0], dims) + (mm(a[0], b[1], dims) + mm(a[1], b[0], dims))


def eye(n):
    return (lax.broadcasted_iota(jnp.int32, (n, n), 0) == lax.broadcasted_iota(jnp.int32, (n, n), 1)).astype(F32)


def inverse_root(gram, frob):
    ident = eye(gram.shape[0])
    scaled = gram / frob
    gap = (0.5 * (ident - scaled)).astype(BF16)
    halves = split(scaled)
    scaled = scaled + (mm(halves[0], gap) + mm(halves[1], gap))
    root = ident + gap.astype(F32)
    for inner in range(1, NS_STEPS):
        upper, lower = split(root), split(scaled)
        gap = (0.5 * (ident - mm3(upper, lower))).astype(BF16)
        root = root + (mm(gap, upper[0]) + mm(gap, upper[1]))
        if inner < NS_STEPS - 1:
            scaled = scaled + (mm(lower[0], gap) + mm(lower[1], gap))
    return split(root)


CHUNKS = [(0, 0, 256), (0, 256, 256), (0, 512, 512), (1, 0, 512), (1, 512, 512), (2, 0, 512), (2, 512, 256), (2, 768, 256)]
AHEAD = 3
ORDER = (2, 1, 3)
LAG = 3
AORDER = (1, 3, 2)


def fit(weights, sources, start, groups, members, capacity):
    held, rows_all, columns = weights.shape
    experts = held * members
    share = rows_all // members
    parts = share // ROW
    part_rows = capacity * ROW
    total = len(CHUNKS)
    depth, rank = start.shape
    rows = parts * part_rows
    chunk = depth // 8
    half = rank // 2
    quarter = half // 4

    def kernel(
        sources_ref, weights_ref, start_ref, basis_ref, coef_ref,
        w_ref, b_ref, proj, proj_t, full, out1, in1, sum1, in2, sum2, in3, root_hi, root_lo, gram_ref, scale_ref,
        start_sem, own_sem, keep_sem, a_send, a_recv, b_send, b_recv, send, recv, *buffers,
    ):
        landed, packed = buffers[:total], buffers[total:]
        g, m = lax.axis_index("grp"), lax.axis_index("mem")
        x, z, c = m // 8, lax.rem(m // 2, 4), lax.rem(m, 2)
        sib = 1 - c
        member = lambda xx, zz, cc: (g, 8 * xx + 2 * zz + cc)
        turn = lambda v, o: lax.rem(v + o, 4)
        others = [(g, m ^ (k ^ (k >> 1))) for k in range(1, members)]
        across = [(lax.rem(g + k, groups), m) for k in range(1, groups)]
        load_start = pltpu.make_async_copy(start_ref, b_ref, start_sem)
        load_start.start()
        greet(others + across)

        def piece(ci, who):
            r, c0, width = CHUNKS[ci]
            return weights_ref.at[:, pl.ds(share * who + ROW * r, ROW), pl.ds(c0, width)]

        def own(ci):
            return pltpu.make_async_copy(piece(ci, m), landed[ci].at[pl.ds(held * m, held)], own_sem.at[ci])

        def launch(ci):
            own(ci).start()
            for dev in others:
                remote(
                    piece(ci, dev[1]), landed[ci].at[pl.ds(held * m, held)], a_send.at[ci], a_recv.at[ci], dev
                ).start()
            landed[ci][experts] = jnp.zeros((ROW, CHUNKS[ci][2]), BF16)

        def target(ci, source_group):
            r, c0, width = CHUNKS[ci]
            return w_ref.at[r, :, pl.ds(pl.multiple_of(columns * source_group + c0, 128), width)]

        def keep(ci):
            return pltpu.make_async_copy(packed[ci].at[g], target(ci, g), keep_sem.at[ci])

        def cross(ci, k):
            dev = across[k - 1]
            return remote(packed[ci].at[dev[0]], target(ci, g), b_send.at[ci, k], b_recv.at[ci, k], dev)

        for ci in range(min(AHEAD, total)):
            launch(ci)
        for ci in range(total):
            own(ci).wait()
            arrivals = landed[ci].at[pl.ds(0, experts - held)]
            pltpu.make_async_copy(arrivals, arrivals, a_recv.at[ci]).wait()

            def pack(k, carry, ci=ci):
                for group in range(groups):
                    packed[ci][group, pl.ds(pl.multiple_of(k * ROW, ROW), ROW), :] = landed[ci][
                        sources_ref[group * capacity + k]
                    ]
                return carry

            lax.fori_loop(0, capacity, pack, 0)
            for k in range(1, groups):
                cross(ci, k).start()
            keep(ci).start()
            if ci + AHEAD < total:
                launch(ci + AHEAD)

        load_start.wait()
        proj[...] = jnp.zeros_like(proj)
        ident = eye(rank).astype(BF16)
        for ci in range(total):
            keep(ci).wait()
            for k in range(1, groups):
                cross(ci, k).wait()
            r, c0, width = CHUNKS[ci]
            at = slice(r * part_rows, (r + 1) * part_rows)
            term = None
            for group in range(groups):
                cols = slice(columns * group + c0, columns * group + c0 + width)
                more = mm(w_ref[r, :, cols], b_ref[cols, :])
                term = more if term is None else term + more
            proj[at, :] += term
            if ci + 1 == total or CHUNKS[ci + 1][0] != r:
                proj_t[:, at] = mm(ident, proj[at, :].astype(BF16), NT).astype(BF16)

        sibling = member(x, z, sib)
        xs = [None] + [member(turn(x, o), z, c) for o in (1, 2, 3)]
        zs = [None] + [member(x, turn(z, o), c) for o in (1, 2, 3)]
        first, second = (xs, zs), (zs, xs)
        place, other = (x, z), (z, x)

        def copy(stage, h, o, src, dst, dev):
            return remote(src, dst, send.at[stage, h, o], recv.at[stage, h, o], dev)

        HALVES = (0, 1)
        steps = [(o, h) for o in ORDER + (0,) for h in HALVES]

        def columns_of(which):
            return pl.ds(pl.multiple_of(which * chunk, chunk), chunk)

        def image_piece(core, q, h):
            total = None
            for r in range(parts):
                term = mm(
                    proj_t[h * half : (h + 1) * half, r * part_rows : (r + 1) * part_rows],
                    w_ref[r, :, columns_of(core * 4 + q)],
                )
                total = term if total is None else total + term
            return total

        def sweep(it, carry):
            ship1, ship2, ship3, ship4, ship5, ship6 = {}, {}, {}, {}, {}, {}

            def give(o, h):
                out1[h, o] = image_piece(sib, turn(place[h], o), h).astype(BF16)
                ship1[o, h] = copy(0, h, o, out1.at[h, o], in1.at[h, o], sibling)
                ship1[o, h].start()

            def take(o, h):
                mine = image_piece(c, turn(place[h], o), h)
                ship1[o, h].wait_recv()
                sum1[h, o] = (mine + in1[h, o].astype(F32)).astype(BF16)
                if o:
                    ship2[o, h] = copy(1, h, o, sum1.at[h, o], in2.at[h, o], first[h][o])
                    ship2[o, h].start()

            for i in range(len(steps) + LAG):
                if i < len(steps):
                    give(*steps[i])
                if i >= LAG:
                    take(*steps[i - LAG])
            for h in HALVES:
                for o in (1, 2, 3):
                    ship2[o, h].wait_recv()
                sum2[h] = (
                    (sum1[h, 0].astype(F32) + in2[h, 1].astype(F32))
                    + (in2[h, 2].astype(F32) + in2[h, 3].astype(F32))
                ).astype(BF16)
                for o in ORDER:
                    rows_there = pl.ds(pl.multiple_of(turn(other[h], o) * quarter, quarter), quarter)
                    ship3[o, h] = copy(2, h, o, sum2.at[h, rows_there], in3.at[h, o], second[h][o])
                    ship3[o, h].start()
            for h in HALVES:
                for o in (1, 2, 3):
                    ship3[o, h].wait_recv()
                mine_rows = pl.ds(pl.multiple_of(other[h] * quarter, quarter), quarter)
                here = pl.ds(pl.multiple_of(h * half + other[h] * quarter, quarter), quarter)
                total = (sum2[h, mine_rows].astype(F32) + in3[h, 1].astype(F32)) + (
                    in3[h, 2].astype(F32) + in3[h, 3].astype(F32)
                )
                spot = full.at[c * 4 + place[h], here]
                full[c * 4 + place[h], here, :] = total.astype(BF16)
                for o in ORDER:
                    ship4[o, h] = copy(3, h, o, spot, spot, second[h][o])
                    ship4[o, h].start()

            def spot_of(core, q, h):
                return full.at[core * 4 + q, pl.ds(h * half, half)]

            def absorb(core, q, h, start):
                cols = slice(h * half, (h + 1) * half)
                block = full[core * 4 + q, h * half : (h + 1) * half, :]
                square = mm(block, block, NT)
                if start:
                    gram_ref[h] = square
                else:
                    gram_ref[h] += square
                for r in range(parts):
                    at = slice(r * part_rows, (r + 1) * part_rows)
                    term = mm(w_ref[r, :, columns_of(core * 4 + q)], block, NT)
                    if start:
                        proj[at, cols] = term
                    else:
                        proj[at, cols] += term

            for h in HALVES:
                for o in (1, 2, 3):
                    ship4[o, h].wait_recv()
                spot = spot_of(c, place[h], h)
                for o in ORDER:
                    ship5[o, h] = copy(4, h, o, spot, spot, first[h][o])
                    ship5[o, h].start()
                ship6[0, h] = copy(5, h, 0, spot, spot, sibling)
                ship6[0, h].start()
            for h in HALVES:
                absorb(c, place[h], h, True)
            for h in HALVES:
                ship6[0, h].wait_recv()
                absorb(sib, place[h], h, False)
            for o in AORDER:
                for h in HALVES:
                    q = turn(place[h], 4 - o)
                    ship5[o, h].wait_recv()
                    spot = spot_of(c, q, h)
                    ship6[o, h] = copy(5, h, o, spot, spot, sibling)
                    ship6[o, h].start()
                for h in HALVES:
                    absorb(c, turn(place[h], 4 - o), h, False)
                for h in HALVES:
                    ship6[o, h].wait_recv()
                    absorb(sib, turn(place[h], 4 - o), h, False)

            cross_gram = None
            for d in range(8):
                term = mm(full[d, 0:half, :], full[d, half:rank, :], NT)
                cross_gram = term if cross_gram is None else cross_gram + term
            gram = jnp.concatenate(
                [
                    jnp.concatenate([gram_ref[0], cross_gram], axis=1),
                    jnp.concatenate([cross_gram.T, gram_ref[1]], axis=1),
                ],
                axis=0,
            )
            frob = jnp.sqrt(jnp.sum(gram * gram)) + 1e-06
            root = inverse_root(gram, frob)
            scale = jnp.sqrt(jnp.float32(depth) / frob)
            root_hi[...] = root[0]
            root_lo[...] = root[1]
            scale_ref[0] = scale

            @pl.when(it + 1 < ITERS)
            def _():
                for r in range(parts):
                    at = slice(r * part_rows, (r + 1) * part_rows)
                    proj_t[:, at] = (mm3(root, split(proj[at, :]), NT) * scale).astype(BF16)

            for o, h in steps:
                ship1[o, h].wait_send()
                ship6[o, h].wait_send()
                if o:
                    for ship in (ship2, ship3, ship4, ship5):
                        ship[o, h].wait_send()
            return carry

        lax.fori_loop(0, ITERS, sweep, 0)

        root = (root_hi[...], root_lo[...])
        scale = scale_ref[0]
        for r in range(parts):
            value = mm3(split(proj[r * part_rows : (r + 1) * part_rows, :]), root) * scale
            coef_ref[:, r * ROW : (r + 1) * ROW, :] = value.astype(BF16).reshape(capacity, ROW, rank)
        block = full[m // 4, :, pl.ds(pl.multiple_of(lax.rem(m, 4) * 128, 128), 128)]
        turned = mm(eye(128).astype(BF16), block, NT).astype(BF16)
        basis_ref[...] = ((mm(turned, root[0]) + mm(turned, root[1])) * scale).astype(BF16)
        for ci in range(total):
            sent = landed[ci].at[pl.ds(0, experts - held)]
            pltpu.make_async_copy(sent, sent, a_send.at[ci]).wait()

    return pl.pallas_call(
        kernel,
        out_shape=(
            jax.ShapeDtypeStruct((128, rank), BF16),
            jax.ShapeDtypeStruct((capacity, parts * ROW, rank), BF16),
        ),
        in_specs=[pl.BlockSpec(memory_space=pltpu.SMEM)] + [pl.BlockSpec(memory_space=pl.ANY)] * 2,
        out_specs=(pl.BlockSpec(memory_space=pltpu.VMEM),) * 2,
        scratch_shapes=[
            pltpu.VMEM((parts, part_rows, depth), BF16),
            pltpu.VMEM((depth, rank), BF16),
            pltpu.VMEM((rows, rank), F32),
            pltpu.VMEM((rank, rows), BF16),
            pltpu.VMEM((8, rank, chunk), BF16),
            pltpu.VMEM((2, 4, half, chunk), BF16),
            pltpu.VMEM((2, 4, half, chunk), BF16),
            pltpu.VMEM((2, 4, half, chunk), BF16),
            pltpu.VMEM((2, 4, half, chunk), BF16),
            pltpu.VMEM((2, half, chunk), BF16),
            pltpu.VMEM((2, 4, quarter, chunk), BF16),
            pltpu.VMEM((rank, rank), BF16),
            pltpu.VMEM((rank, rank), BF16),
            pltpu.VMEM((2, half, half), F32),
            pltpu.SMEM((1,), F32),
            pltpu.SemaphoreType.DMA,
            pltpu.SemaphoreType.DMA((total,)),
            pltpu.SemaphoreType.DMA((total,)),
            pltpu.SemaphoreType.DMA((total,)),
            pltpu.SemaphoreType.DMA((total,)),
            pltpu.SemaphoreType.DMA((total, groups)),
            pltpu.SemaphoreType.DMA((total, groups)),
            pltpu.SemaphoreType.DMA((6, 2, 4)),
            pltpu.SemaphoreType.DMA((6, 2, 4)),
        ]
        + [pltpu.VMEM((experts + 1, ROW, width), BF16) for _, _, width in CHUNKS]
        + [pltpu.VMEM((groups, part_rows, width), BF16) for _, _, width in CHUNKS],
        compiler_params=pltpu.CompilerParams(
            collective_id=0, has_side_effects=True, vmem_limit_bytes=VMEM_LIMIT
        ),
        cost_estimate=pl.CostEstimate(flops=60 << 30, bytes_accessed=16 << 20, transcendentals=0),
        name="fit",
    )(sources, weights, start)


def body(weights, stored_order, assignment, init_basis):
    groups, members = lax.axis_size("grp"), lax.axis_size("mem")
    experts = weights.shape[0] * members
    capacity = experts // groups + experts // (2 * groups)
    sources = slot_sources(stored_order, assignment, groups, capacity)
    basis, coefficients = fit(weights, sources, init_basis[0], groups, members, capacity)
    return (basis[None], coefficients[None])


def solution(mesh):
    return jax.shard_map(
        body,
        mesh=mesh,
        in_specs=(P("mem", None, "grp"), P(), P(), P("grp", None, None)),
        out_specs=(P("grp", "mem", None), P("grp", None, "mem", None)),
        check_vma=False,
    )
```

```python
import jax
import jax.numpy as jnp
from jax import lax
from jax.experimental import pallas as pl
from jax.experimental.pallas import tpu as pltpu
from jax.sharding import PartitionSpec as P

ITERS = 2
NS_STEPS = 6
MESH = pl.DeviceIdType.MESH
F32 = jnp.float32
BF16 = jnp.bfloat16
ROW = 16
VMEM_LIMIT = 60 * 1024 * 1024


def remote(src, dst, send, recv, device):
    return pltpu.make_async_remote_copy(
        src_ref=src, dst_ref=dst, send_sem=send, recv_sem=recv, device_id=device, device_id_type=MESH
    )


def greet(peers):
    barrier = pltpu.get_barrier_semaphore()
    for peer in peers:
        pl.semaphore_signal(barrier, inc=1, device_id=peer, device_id_type=MESH)
    pl.semaphore_wait(barrier, len(peers))


def slot_sources(stored_order, assignment, groups, capacity):
    assign = assignment[:, 0]
    experts = assign.shape[0]
    ids = jnp.arange(experts, dtype=jnp.int32)
    same = (assign[None, :] == assign[:, None]) & (ids[None, :] < ids[:, None])
    slot = assign * capacity + jnp.sum(same.astype(jnp.int32), axis=1)
    held = (stored_order[:, None] == ids[None, :]).astype(jnp.int32)
    slot_of_position = jnp.sum(held * slot[None, :], axis=1)
    slots = jnp.arange(groups * capacity, dtype=jnp.int32)
    hit = (slot_of_position[None, :] == slots[:, None]).astype(jnp.int32)
    return experts + jnp.sum(hit * (ids - experts)[None, :], axis=1)


NN = (((1,), (0,)), ((), ()))
NT = (((1,), (1,)), ((), ()))


def mm(a, b, dims=NN):
    return lax.dot_general(a, b, dims, preferred_element_type=F32)


def split(x):
    high = x.astype(BF16)
    return high, (x - high.astype(F32)).astype(BF16)


def mm3(a, b, dims=NN):
    return mm(a[0], b[0], dims) + (mm(a[0], b[1], dims) + mm(a[1], b[0], dims))


def eye(n):
    return (lax.broadcasted_iota(jnp.int32, (n, n), 0) == lax.broadcasted_iota(jnp.int32, (n, n), 1)).astype(F32)


def inverse_root(gram, frob):
    ident = eye(gram.shape[0])
    scaled = gram / frob
    gap = (0.5 * (ident - scaled)).astype(BF16)
    halves = split(scaled)
    scaled = scaled + (mm(halves[0], gap) + mm(halves[1], gap))
    root = ident + gap.astype(F32)
    for inner in range(1, NS_STEPS):
        upper, lower = split(root), split(scaled)
        gap = (0.5 * (ident - mm3(upper, lower))).astype(BF16)
        root = root + (mm(gap, upper[0]) + mm(gap, upper[1]))
        if inner < NS_STEPS - 1:
            scaled = scaled + (mm(lower[0], gap) + mm(lower[1], gap))
    return split(root)


CHUNKS = [(0, 0, 256), (0, 256, 256), (0, 512, 512), (1, 0, 512), (1, 512, 512), (2, 0, 512), (2, 512, 256), (2, 768, 256)]
AHEAD = 3
ORDER = (2, 1, 3)
LAG = 3
CUTS = 2
AORDER = (1, 3, 2)


def fit(weights, sources, start, groups, members, capacity):
    held, rows_all, columns = weights.shape
    experts = held * members
    share = rows_all // members
    parts = share // ROW
    part_rows = capacity * ROW
    total = len(CHUNKS)
    depth, rank = start.shape
    rows = parts * part_rows
    chunk = depth // 8 // CUTS
    half = rank // 2
    quarter = half // 4

    def kernel(
        sources_ref, weights_ref, start_ref, basis_ref, coef_ref,
        w_ref, b_ref, proj, proj_t, full, out1, in1, sum1, in2, sum2, in3, root_hi, root_lo, gram_ref, scale_ref,
        start_sem, own_sem, keep_sem, a_send, a_recv, b_send, b_recv, send, recv, *buffers,
    ):
        landed, packed = buffers[:total], buffers[total:]
        g, m = lax.axis_index("grp"), lax.axis_index("mem")
        x, z, c = m // 8, lax.rem(m // 2, 4), lax.rem(m, 2)
        sib = 1 - c
        member = lambda xx, zz, cc: (g, 8 * xx + 2 * zz + cc)
        turn = lambda v, o: lax.rem(v + o, 4)
        others = [(g, m ^ (k ^ (k >> 1))) for k in range(1, members)]
        across = [(lax.rem(g + k, groups), m) for k in range(1, groups)]
        load_start = pltpu.make_async_copy(start_ref, b_ref, start_sem)
        load_start.start()
        greet(others + across)

        def piece(ci, who):
            r, c0, width = CHUNKS[ci]
            return weights_ref.at[:, pl.ds(share * who + ROW * r, ROW), pl.ds(c0, width)]

        def own(ci):
            return pltpu.make_async_copy(piece(ci, m), landed[ci].at[pl.ds(held * m, held)], own_sem.at[ci])

        def launch(ci):
            own(ci).start()
            for dev in others:
                remote(
                    piece(ci, dev[1]), landed[ci].at[pl.ds(held * m, held)], a_send.at[ci], a_recv.at[ci], dev
                ).start()
            landed[ci][experts] = jnp.zeros((ROW, CHUNKS[ci][2]), BF16)

        def target(ci, source_group):
            r, c0, width = CHUNKS[ci]
            return w_ref.at[pl.ds(r * part_rows, part_rows), pl.ds(pl.multiple_of(columns * source_group + c0, 128), width)]

        def keep(ci):
            return pltpu.make_async_copy(packed[ci].at[g], target(ci, g), keep_sem.at[ci])

        def cross(ci, k):
            dev = across[k - 1]
            return remote(packed[ci].at[dev[0]], target(ci, g), b_send.at[ci, k], b_recv.at[ci, k], dev)

        for ci in range(min(AHEAD, total)):
            launch(ci)
        for ci in range(total):
            own(ci).wait()
            arrivals = landed[ci].at[pl.ds(0, experts - held)]
            pltpu.make_async_copy(arrivals, arrivals, a_recv.at[ci]).wait()

            def pack(k, carry, ci=ci):
                for group in range(groups):
                    packed[ci][group, pl.ds(pl.multiple_of(k * ROW, ROW), ROW), :] = landed[ci][
                        sources_ref[group * capacity + k]
                    ]
                return carry

            lax.fori_loop(0, capacity, pack, 0)
            for k in range(1, groups):
                cross(ci, k).start()
            keep(ci).start()
            if ci + AHEAD < total:
                launch(ci + AHEAD)

        load_start.wait()
        proj[...] = jnp.zeros_like(proj)
        ident = eye(rank).astype(BF16)
        for ci in range(total):
            keep(ci).wait()
            for k in range(1, groups):
                cross(ci, k).wait()
            r, c0, width = CHUNKS[ci]
            at = slice(r * part_rows, (r + 1) * part_rows)
            term = None
            for group in range(groups):
                cols = slice(columns * group + c0, columns * group + c0 + width)
                more = mm(w_ref[at, cols], b_ref[cols, :])
                term = more if term is None else term + more
            proj[at, :] += term
            if ci + 1 == total or CHUNKS[ci + 1][0] != r:
                proj_t[:, at] = mm(ident, proj[at, :].astype(BF16), NT).astype(BF16)

        sibling = member(x, z, sib)
        xs = [None] + [member(turn(x, o), z, c) for o in (1, 2, 3)]
        zs = [None] + [member(x, turn(z, o), c) for o in (1, 2, 3)]
        first, second = (xs, zs), (zs, xs)
        place, other = (x, z), (z, x)

        def copy(stage, h, u, o, src, dst, dev):
            return remote(src, dst, send.at[stage, h, u, o], recv.at[stage, h, u, o], dev)

        HALVES = (0, 1)
        steps = [(u, o, h) for u in range(CUTS) for o in ORDER + (0,) for h in HALVES]

        def index_of(core, q, u):
            return (core * 4 + q) * CUTS + u

        def columns_of(core, q, u):
            return pl.ds(pl.multiple_of(index_of(core, q, u) * chunk, chunk), chunk)

        def image_piece(core, q, u, h):
            left = proj_t.at[pl.ds(h * half, half)]
            cols = columns_of(core, q, u)
            cut = rows // 256 * 256
            return mm(left[:, 0:cut], w_ref[0:cut, cols]) + mm(left[:, cut:rows], w_ref[cut:rows, cols])

        def sweep(it, carry):
            ship1, ship2, ship3, ship4, ship5, ship6 = {}, {}, {}, {}, {}, {}

            def give(u, o, h):
                out1[h, u, o] = image_piece(sib, turn(place[h], o), u, h).astype(BF16)
                ship1[u, o, h] = copy(0, h, u, o, out1.at[h, u, o], in1.at[h, u, o], sibling)
                ship1[u, o, h].start()

            def take(u, o, h):
                mine = image_piece(c, turn(place[h], o), u, h)
                ship1[u, o, h].wait_recv()
                sum1[h, u, o] = (mine + in1[h, u, o].astype(F32)).astype(BF16)
                if o:
                    ship2[u, o, h] = copy(1, h, u, o, sum1.at[h, u, o], in2.at[h, u, o], first[h][o])
                    ship2[u, o, h].start()

            def sum_first(u):
                for h in HALVES:
                    for o in (1, 2, 3):
                        ship2[u, o, h].wait_recv()
                    sum2[h, u] = (
                        (sum1[h, u, 0].astype(F32) + in2[h, u, 1].astype(F32))
                        + (in2[h, u, 2].astype(F32) + in2[h, u, 3].astype(F32))
                    ).astype(BF16)
                    for o in ORDER:
                        rows_there = pl.ds(pl.multiple_of(turn(other[h], o) * quarter, quarter), quarter)
                        ship3[u, o, h] = copy(2, h, u, o, sum2.at[h, u, rows_there], in3.at[h, u, o], second[h][o])
                        ship3[u, o, h].start()

            def sum_second(u):
                for h in HALVES:
                    for o in (1, 2, 3):
                        ship3[u, o, h].wait_recv()
                    mine_rows = pl.ds(pl.multiple_of(other[h] * quarter, quarter), quarter)
                    here = pl.ds(pl.multiple_of(h * half + other[h] * quarter, quarter), quarter)
                    total = (sum2[h, u, mine_rows].astype(F32) + in3[h, u, 1].astype(F32)) + (
                        in3[h, u, 2].astype(F32) + in3[h, u, 3].astype(F32)
                    )
                    at = index_of(c, place[h], u)
                    full[at, here, :] = total.astype(BF16)
                    for o in ORDER:
                        spot = full.at[at, here]
                        ship4[u, o, h] = copy(3, h, u, o, spot, spot, second[h][o])
                        ship4[u, o, h].start()

            def origin(o, h):
                return turn(place[h], (4 - o) % 4)

            def hand_over(u, o, h):
                spot = full.at[index_of(c, origin(o, h), u), pl.ds(h * half, half)]
                ship6[u, o, h] = copy(5, h, u, o, spot, spot, sibling)
                ship6[u, o, h].start()

            def spread(u):
                for h in HALVES:
                    for o in (1, 2, 3):
                        ship4[u, o, h].wait_recv()
                    spot = full.at[index_of(c, place[h], u), pl.ds(h * half, half)]
                    hand_over(u, 0, h)
                    for o in ORDER:
                        ship5[u, o, h] = copy(4, h, u, o, spot, spot, first[h][o])
                        ship5[u, o, h].start()

            def collect(u, o):
                for h in HALVES:
                    ship5[u, o, h].wait_recv()
                    hand_over(u, o, h)

            def absorb(u, o, start=False):
                for h in HALVES:
                    ship6[u, o, h].wait_recv()
                    cols = slice(h * half, (h + 1) * half)
                    q = origin(o, h)
                    blocks = [full[index_of(core, q, u), h * half : (h + 1) * half, :] for core in (c, sib)]
                    square = mm(blocks[0], blocks[0], NT) + mm(blocks[1], blocks[1], NT)
                    if start:
                        gram_ref[h] = square
                    else:
                        gram_ref[h] += square
                    for r in range(0, rows, part_rows):
                        at = slice(r, r + part_rows)
                        term = mm(w_ref[at, columns_of(c, q, u)], blocks[0], NT) + mm(
                            w_ref[at, columns_of(sib, q, u)], blocks[1], NT
                        )
                        if start:
                            proj[at, cols] = term
                        else:
                            proj[at, cols] += term

            for i in range(len(steps) + LAG):
                if i < len(steps):
                    give(*steps[i])
                if i >= LAG:
                    take(*steps[i - LAG])
            sum_first(0)
            for u in range(CUTS):
                sum_second(u)
                if u + 1 < CUTS:
                    sum_first(u + 1)
                spread(u)
            waiting = []
            for u in range(CUTS):
                waiting.append((u, 0))
            absorb(0, 0, True)
            waiting = waiting[1:]
            for u in range(CUTS):
                for o in AORDER:
                    collect(u, o)
                    waiting.append((u, o))
                    absorb(*waiting.pop(0))
            for item in waiting:
                absorb(*item)

            cross_gram = None
            for d in range(8 * CUTS):
                term = mm(full[d, 0:half, :], full[d, half:rank, :], NT)
                cross_gram = term if cross_gram is None else cross_gram + term
            gram = jnp.concatenate(
                [
                    jnp.concatenate([gram_ref[0], cross_gram], axis=1),
                    jnp.concatenate([cross_gram.T, gram_ref[1]], axis=1),
                ],
                axis=0,
            )
            frob = jnp.sqrt(jnp.sum(gram * gram)) + 1e-06
            root = inverse_root(gram, frob)
            scale = jnp.sqrt(jnp.float32(depth) / frob)
            root_hi[...] = root[0]
            root_lo[...] = root[1]
            scale_ref[0] = scale

            @pl.when(it + 1 < ITERS)
            def _():
                proj_t[...] = (mm3(root, split(proj[...]), NT) * scale).astype(BF16)

            for step in steps:
                ship1[step].wait_send()
                ship6[step].wait_send()
                if step[1]:
                    for ship in (ship2, ship3, ship4, ship5):
                        ship[step].wait_send()
            return carry

        lax.fori_loop(0, ITERS, sweep, 0)

        root = (root_hi[...], root_lo[...])
        scale = scale_ref[0]
        for r in range(parts):
            value = mm3(split(proj[r * part_rows : (r + 1) * part_rows, :]), root) * scale
            coef_ref[:, r * ROW : (r + 1) * ROW, :] = value.astype(BF16).reshape(capacity, ROW, rank)
        per = chunk // 128
        block = full[m // per, :, pl.ds(pl.multiple_of(lax.rem(m, per) * 128, 128), 128)]
        turned = mm(eye(128).astype(BF16), block, NT).astype(BF16)
        basis_ref[...] = ((mm(turned, root[0]) + mm(turned, root[1])) * scale).astype(BF16)
        for ci in range(total):
            sent = landed[ci].at[pl.ds(0, experts - held)]
            pltpu.make_async_copy(sent, sent, a_send.at[ci]).wait()

    return pl.pallas_call(
        kernel,
        out_shape=(
            jax.ShapeDtypeStruct((128, rank), BF16),
            jax.ShapeDtypeStruct((capacity, parts * ROW, rank), BF16),
        ),
        in_specs=[pl.BlockSpec(memory_space=pltpu.SMEM)] + [pl.BlockSpec(memory_space=pl.ANY)] * 2,
        out_specs=(pl.BlockSpec(memory_space=pltpu.VMEM),) * 2,
        scratch_shapes=[
            pltpu.VMEM((rows, depth), BF16),
            pltpu.VMEM((depth, rank), BF16),
            pltpu.VMEM((rows, rank), F32),
            pltpu.VMEM((rank, rows), BF16),
            pltpu.VMEM((8 * CUTS, rank, chunk), BF16),
            pltpu.VMEM((2, CUTS, 4, half, chunk), BF16),
            pltpu.VMEM((2, CUTS, 4, half, chunk), BF16),
            pltpu.VMEM((2, CUTS, 4, half, chunk), BF16),
            pltpu.VMEM((2, CUTS, 4, half, chunk), BF16),
            pltpu.VMEM((2, CUTS, half, chunk), BF16),
            pltpu.VMEM((2, CUTS, 4, quarter, chunk), BF16),
            pltpu.VMEM((rank, rank), BF16),
            pltpu.VMEM((rank, rank), BF16),
            pltpu.VMEM((2, half, half), F32),
            pltpu.SMEM((1,), F32),
            pltpu.SemaphoreType.DMA,
            pltpu.SemaphoreType.DMA((total,)),
            pltpu.SemaphoreType.DMA((total,)),
            pltpu.SemaphoreType.DMA((total,)),
            pltpu.SemaphoreType.DMA((total,)),
            pltpu.SemaphoreType.DMA((total, groups)),
            pltpu.SemaphoreType.DMA((total, groups)),
            pltpu.SemaphoreType.DMA((6, 2, CUTS, 4)),
            pltpu.SemaphoreType.DMA((6, 2, CUTS, 4)),
        ]
        + [pltpu.VMEM((experts + 1, ROW, width), BF16) for _, _, width in CHUNKS]
        + [pltpu.VMEM((groups, part_rows, width), BF16) for _, _, width in CHUNKS],
        compiler_params=pltpu.CompilerParams(
            collective_id=0, has_side_effects=True, vmem_limit_bytes=VMEM_LIMIT
        ),
        cost_estimate=pl.CostEstimate(flops=60 << 30, bytes_accessed=16 << 20, transcendentals=0),
        name="fit",
    )(sources, weights, start)


def body(weights, stored_order, assignment, init_basis):
    groups, members = lax.axis_size("grp"), lax.axis_size("mem")
    experts = weights.shape[0] * members
    capacity = experts // groups + experts // (2 * groups)
    sources = slot_sources(stored_order, assignment, groups, capacity)
    basis, coefficients = fit(weights, sources, init_basis[0], groups, members, capacity)
    return (basis[None], coefficients[None])


def solution(mesh):
    return jax.shard_map(
        body,
        mesh=mesh,
        in_specs=(P("mem", None, "grp"), P(), P(), P("grp", None, None)),
        out_specs=(P("grp", "mem", None), P("grp", None, "mem", None)),
        check_vma=False,
    )
```

```python
import jax
import jax.numpy as jnp
from jax import lax
from jax.experimental import pallas as pl
from jax.experimental.pallas import tpu as pltpu
from jax.sharding import PartitionSpec as P

ITERS = 2
NS_STEPS = 6
MESH = pl.DeviceIdType.MESH
F32 = jnp.float32
BF16 = jnp.bfloat16
ROW = 16
VMEM_LIMIT = 60 * 1024 * 1024


def remote(src, dst, send, recv, device):
    return pltpu.make_async_remote_copy(
        src_ref=src, dst_ref=dst, send_sem=send, recv_sem=recv, device_id=device, device_id_type=MESH
    )


def greet(peers):
    barrier = pltpu.get_barrier_semaphore()
    for peer in peers:
        pl.semaphore_signal(barrier, inc=1, device_id=peer, device_id_type=MESH)
    pl.semaphore_wait(barrier, len(peers))


def slot_sources(stored_order, assignment, groups, capacity):
    assign = assignment[:, 0]
    experts = assign.shape[0]
    ids = jnp.arange(experts, dtype=jnp.int32)
    before = (assign[None, :] == assign[:, None]) & (ids[None, :] < ids[:, None])
    whole = jnp.where(ids[None, :] < assign[:, None], capacity, 0)
    slot = jnp.sum(whole + before.astype(jnp.int32), axis=1)
    slot_of_position = jnp.sum(jnp.where(stored_order[:, None] == ids[None, :], slot[None, :], 0), axis=1)
    slots = jnp.arange(groups * capacity, dtype=jnp.int32)
    return jnp.min(jnp.where(slot_of_position[None, :] == slots[:, None], ids[None, :], experts), axis=1)


NN = (((1,), (0,)), ((), ()))
NT = (((1,), (1,)), ((), ()))


def mm(a, b, dims=NN):
    return lax.dot_general(a, b, dims, preferred_element_type=F32)


def split(x):
    high = x.astype(BF16)
    return high, (x - high.astype(F32)).astype(BF16)


def mm3(a, b, dims=NN):
    return mm(a[0], b[0], dims) + (mm(a[0], b[1], dims) + mm(a[1], b[0], dims))


def eye(n):
    return (lax.broadcasted_iota(jnp.int32, (n, n), 0) == lax.broadcasted_iota(jnp.int32, (n, n), 1)).astype(F32)


def inverse_root(gram, frob):
    ident = eye(gram.shape[0])
    scaled = gram / frob
    gap = (0.5 * (ident - scaled)).astype(BF16)
    halves = split(scaled)
    scaled = scaled + (mm(halves[0], gap) + mm(halves[1], gap))
    root = ident + gap.astype(F32)
    for inner in range(1, NS_STEPS):
        upper, lower = split(root), split(scaled)
        gap = (0.5 * (ident - mm3(upper, lower))).astype(BF16)
        root = root + (mm(gap, upper[0]) + mm(gap, upper[1]))
        if inner < NS_STEPS - 1:
            scaled = scaled + (mm(lower[0], gap) + mm(lower[1], gap))
    return split(root)


CHUNKS = [(0, 0, 256), (0, 256, 256), (0, 512, 512), (1, 0, 512), (1, 512, 512), (2, 0, 512), (2, 512, 256), (2, 768, 256)]
AHEAD = 3
ORDER = (2, 1, 3)
LAG = 3
CUTS = 2
AORDER = (1, 3, 2)


def fit(weights, sources, start, groups, members, capacity):
    held, rows_all, columns = weights.shape
    experts = held * members
    share = rows_all // members
    parts = share // ROW
    part_rows = capacity * ROW
    total = len(CHUNKS)
    depth, rank = start.shape
    rows = parts * part_rows
    chunk = depth // 8 // CUTS
    half = rank // 2
    quarter = half // 4

    def kernel(
        sources_ref, weights_ref, start_ref, basis_ref, coef_ref,
        w_ref, b_ref, proj, proj_t, full, out1, in1, sum1, in2, sum2, in3, root_hi, root_lo, gram_ref, scale_ref,
        start_sem, own_sem, keep_sem, a_send, a_recv, b_send, b_recv, send, recv, *buffers,
    ):
        landed, packed = buffers[:total], buffers[total:]
        g, m = lax.axis_index("grp"), lax.axis_index("mem")
        x, z, c = m // 8, lax.rem(m // 2, 4), lax.rem(m, 2)
        sib = 1 - c
        member = lambda xx, zz, cc: (g, 8 * xx + 2 * zz + cc)
        turn = lambda v, o: lax.rem(v + o, 4)
        others = [(g, m ^ (k ^ (k >> 1))) for k in range(1, members)]
        across = [(lax.rem(g + k, groups), m) for k in range(1, groups)]
        load_start = pltpu.make_async_copy(start_ref, b_ref, start_sem)
        load_start.start()
        greet(others + across)

        def piece(ci, who):
            r, c0, width = CHUNKS[ci]
            return weights_ref.at[:, pl.ds(share * who + ROW * r, ROW), pl.ds(c0, width)]

        def own(ci):
            return pltpu.make_async_copy(piece(ci, m), landed[ci].at[pl.ds(held * m, held)], own_sem.at[ci])

        def launch(ci):
            own(ci).start()
            for dev in others:
                remote(
                    piece(ci, dev[1]), landed[ci].at[pl.ds(held * m, held)], a_send.at[ci], a_recv.at[ci], dev
                ).start()
            landed[ci][experts] = jnp.zeros((ROW, CHUNKS[ci][2]), BF16)

        def target(ci, source_group):
            r, c0, width = CHUNKS[ci]
            return w_ref.at[pl.ds(r * part_rows, part_rows), pl.ds(pl.multiple_of(columns * source_group + c0, 128), width)]

        def keep(ci):
            return pltpu.make_async_copy(packed[ci].at[g], target(ci, g), keep_sem.at[ci])

        def cross(ci, k):
            dev = across[k - 1]
            return remote(packed[ci].at[dev[0]], target(ci, g), b_send.at[ci, k], b_recv.at[ci, k], dev)

        for ci in range(min(AHEAD, total)):
            launch(ci)
        for ci in range(total):
            own(ci).wait()
            arrivals = landed[ci].at[pl.ds(0, experts - held)]
            pltpu.make_async_copy(arrivals, arrivals, a_recv.at[ci]).wait()

            def pack(k, carry, ci=ci):
                for group in range(groups):
                    packed[ci][group, pl.ds(pl.multiple_of(k * ROW, ROW), ROW), :] = landed[ci][
                        sources_ref[group * capacity + k]
                    ]
                return carry

            lax.fori_loop(0, capacity, pack, 0)
            for k in range(1, groups):
                cross(ci, k).start()
            keep(ci).start()
            if ci + AHEAD < total:
                launch(ci + AHEAD)

        load_start.wait()
        proj[...] = jnp.zeros_like(proj)
        ident = eye(rank).astype(BF16)
        for ci in range(total):
            keep(ci).wait()
            for k in range(1, groups):
                cross(ci, k).wait()
            r, c0, width = CHUNKS[ci]
            at = slice(r * part_rows, (r + 1) * part_rows)
            term = None
            for group in range(groups):
                cols = slice(columns * group + c0, columns * group + c0 + width)
                more = mm(w_ref[at, cols], b_ref[cols, :])
                term = more if term is None else term + more
            proj[at, :] += term
            if ci + 1 == total or CHUNKS[ci + 1][0] != r:
                proj_t[:, at] = mm(ident, proj[at, :].astype(BF16), NT).astype(BF16)

        sibling = member(x, z, sib)
        xs = [None] + [member(turn(x, o), z, c) for o in (1, 2, 3)]
        zs = [None] + [member(x, turn(z, o), c) for o in (1, 2, 3)]
        first, second = (xs, zs), (zs, xs)
        place, other = (x, z), (z, x)

        def copy(stage, h, u, o, src, dst, dev):
            return remote(src, dst, send.at[stage, h, u, o], recv.at[stage, h, u, o], dev)

        HALVES = (0, 1)
        steps = [(u, o, h) for u in range(CUTS) for o in ORDER + (0,) for h in HALVES]

        def index_of(core, q, u):
            return (core * 4 + q) * CUTS + u

        def columns_of(core, q, u):
            return pl.ds(pl.multiple_of(index_of(core, q, u) * chunk, chunk), chunk)

        def image_piece(core, q, u, h):
            left = proj_t.at[pl.ds(h * half, half)]
            cols = columns_of(core, q, u)
            cut = rows // 256 * 256
            return mm(left[:, 0:cut], w_ref[0:cut, cols]) + mm(left[:, cut:rows], w_ref[cut:rows, cols])

        def sweep(it, carry):
            ship1, ship2, ship3, ship4, ship5, ship6 = {}, {}, {}, {}, {}, {}

            def give(u, o, h):
                out1[h, u, o] = image_piece(sib, turn(place[h], o), u, h).astype(BF16)
                ship1[u, o, h] = copy(0, h, u, o, out1.at[h, u, o], in1.at[h, u, o], sibling)
                ship1[u, o, h].start()

            def take(u, o, h):
                mine = image_piece(c, turn(place[h], o), u, h)
                ship1[u, o, h].wait_recv()
                sum1[h, u, o] = (mine + in1[h, u, o].astype(F32)).astype(BF16)
                if o:
                    ship2[u, o, h] = copy(1, h, u, o, sum1.at[h, u, o], in2.at[h, u, o], first[h][o])
                    ship2[u, o, h].start()

            def sum_first(u):
                for h in HALVES:
                    for o in (1, 2, 3):
                        ship2[u, o, h].wait_recv()
                    sum2[h, u] = (
                        (sum1[h, u, 0].astype(F32) + in2[h, u, 1].astype(F32))
                        + (in2[h, u, 2].astype(F32) + in2[h, u, 3].astype(F32))
                    ).astype(BF16)
                    for o in ORDER:
                        rows_there = pl.ds(pl.multiple_of(turn(other[h], o) * quarter, quarter), quarter)
                        ship3[u, o, h] = copy(2, h, u, o, sum2.at[h, u, rows_there], in3.at[h, u, o], second[h][o])
                        ship3[u, o, h].start()

            def sum_second(u):
                for h in HALVES:
                    for o in (1, 2, 3):
                        ship3[u, o, h].wait_recv()
                    mine_rows = pl.ds(pl.multiple_of(other[h] * quarter, quarter), quarter)
                    here = pl.ds(pl.multiple_of(h * half + other[h] * quarter, quarter), quarter)
                    total = (sum2[h, u, mine_rows].astype(F32) + in3[h, u, 1].astype(F32)) + (
                        in3[h, u, 2].astype(F32) + in3[h, u, 3].astype(F32)
                    )
                    at = index_of(c, place[h], u)
                    full[at, here, :] = total.astype(BF16)
                    for o in ORDER:
                        spot = full.at[at, here]
                        ship4[u, o, h] = copy(3, h, u, o, spot, spot, second[h][o])
                        ship4[u, o, h].start()

            def origin(o, h):
                return turn(place[h], (4 - o) % 4)

            def hand_over(u, o, h):
                spot = full.at[index_of(c, origin(o, h), u), pl.ds(h * half, half)]
                ship6[u, o, h] = copy(5, h, u, o, spot, spot, sibling)
                ship6[u, o, h].start()

            def spread(u):
                for h in HALVES:
                    for o in (1, 2, 3):
                        ship4[u, o, h].wait_recv()
                    spot = full.at[index_of(c, place[h], u), pl.ds(h * half, half)]
                    hand_over(u, 0, h)
                    for o in ORDER:
                        ship5[u, o, h] = copy(4, h, u, o, spot, spot, first[h][o])
                        ship5[u, o, h].start()

            def collect(u, o):
                for h in HALVES:
                    ship5[u, o, h].wait_recv()
                    hand_over(u, o, h)

            def absorb(u, o, start=False):
                for h in HALVES:
                    ship6[u, o, h].wait_recv()
                    cols = slice(h * half, (h + 1) * half)
                    q = origin(o, h)
                    blocks = [full[index_of(core, q, u), h * half : (h + 1) * half, :] for core in (c, sib)]
                    square = mm(blocks[0], blocks[0], NT) + mm(blocks[1], blocks[1], NT)
                    if start:
                        gram_ref[h] = square
                    else:
                        gram_ref[h] += square
                    for r in range(0, rows, part_rows):
                        at = slice(r, r + part_rows)
                        term = mm(w_ref[at, columns_of(c, q, u)], blocks[0], NT) + mm(
                            w_ref[at, columns_of(sib, q, u)], blocks[1], NT
                        )
                        if start:
                            proj[at, cols] = term
                        else:
                            proj[at, cols] += term

            for i in range(len(steps) + LAG):
                if i < len(steps):
                    give(*steps[i])
                if i >= LAG:
                    take(*steps[i - LAG])
            sum_first(0)
            for u in range(CUTS):
                sum_second(u)
                if u + 1 < CUTS:
                    sum_first(u + 1)
                spread(u)
            waiting = []
            for u in range(CUTS):
                waiting.append((u, 0))
            absorb(0, 0, True)
            waiting = waiting[1:]
            for u in range(CUTS):
                for o in AORDER:
                    collect(u, o)
                    waiting.append((u, o))
                    absorb(*waiting.pop(0))
            for item in waiting:
                absorb(*item)

            cross_gram = None
            for d in range(8 * CUTS):
                term = mm(full[d, 0:half, :], full[d, half:rank, :], NT)
                cross_gram = term if cross_gram is None else cross_gram + term
            gram = jnp.concatenate(
                [
                    jnp.concatenate([gram_ref[0], cross_gram], axis=1),
                    jnp.concatenate([cross_gram.T, gram_ref[1]], axis=1),
                ],
                axis=0,
            )
            frob = jnp.sqrt(jnp.sum(gram * gram)) + 1e-06
            root = inverse_root(gram, frob)
            scale = jnp.sqrt(jnp.float32(depth) / frob)
            root_hi[...] = root[0]
            root_lo[...] = root[1]
            scale_ref[0] = scale

            @pl.when(it + 1 < ITERS)
            def _():
                proj_t[...] = (mm3(root, split(proj[...]), NT) * scale).astype(BF16)

            for step in steps:
                ship1[step].wait_send()
                ship6[step].wait_send()
                if step[1]:
                    for ship in (ship2, ship3, ship4, ship5):
                        ship[step].wait_send()
            return carry

        lax.fori_loop(0, ITERS, sweep, 0)

        root = (root_hi[...], root_lo[...])
        scale = scale_ref[0]
        for r in range(parts):
            value = mm3(split(proj[r * part_rows : (r + 1) * part_rows, :]), root) * scale
            coef_ref[:, r * ROW : (r + 1) * ROW, :] = value.astype(BF16).reshape(capacity, ROW, rank)
        per = chunk // 128
        block = full[m // per, :, pl.ds(pl.multiple_of(lax.rem(m, per) * 128, 128), 128)]
        turned = mm(eye(128).astype(BF16), block, NT).astype(BF16)
        basis_ref[...] = ((mm(turned, root[0]) + mm(turned, root[1])) * scale).astype(BF16)
        for ci in range(total):
            sent = landed[ci].at[pl.ds(0, experts - held)]
            pltpu.make_async_copy(sent, sent, a_send.at[ci]).wait()

    return pl.pallas_call(
        kernel,
        out_shape=(
            jax.ShapeDtypeStruct((128, rank), BF16),
            jax.ShapeDtypeStruct((capacity, parts * ROW, rank), BF16),
        ),
        in_specs=[pl.BlockSpec(memory_space=pltpu.SMEM)] + [pl.BlockSpec(memory_space=pl.ANY)] * 2,
        out_specs=(pl.BlockSpec(memory_space=pltpu.VMEM),) * 2,
        scratch_shapes=[
            pltpu.VMEM((rows, depth), BF16),
            pltpu.VMEM((depth, rank), BF16),
            pltpu.VMEM((rows, rank), F32),
            pltpu.VMEM((rank, rows), BF16),
            pltpu.VMEM((8 * CUTS, rank, chunk), BF16),
            pltpu.VMEM((2, CUTS, 4, half, chunk), BF16),
            pltpu.VMEM((2, CUTS, 4, half, chunk), BF16),
            pltpu.VMEM((2, CUTS, 4, half, chunk), BF16),
            pltpu.VMEM((2, CUTS, 4, half, chunk), BF16),
            pltpu.VMEM((2, CUTS, half, chunk), BF16),
            pltpu.VMEM((2, CUTS, 4, quarter, chunk), BF16),
            pltpu.VMEM((rank, rank), BF16),
            pltpu.VMEM((rank, rank), BF16),
            pltpu.VMEM((2, half, half), F32),
            pltpu.SMEM((1,), F32),
            pltpu.SemaphoreType.DMA,
            pltpu.SemaphoreType.DMA((total,)),
            pltpu.SemaphoreType.DMA((total,)),
            pltpu.SemaphoreType.DMA((total,)),
            pltpu.SemaphoreType.DMA((total,)),
            pltpu.SemaphoreType.DMA((total, groups)),
            pltpu.SemaphoreType.DMA((total, groups)),
            pltpu.SemaphoreType.DMA((6, 2, CUTS, 4)),
            pltpu.SemaphoreType.DMA((6, 2, CUTS, 4)),
        ]
        + [pltpu.VMEM((experts + 1, ROW, width), BF16) for _, _, width in CHUNKS]
        + [pltpu.VMEM((groups, part_rows, width), BF16) for _, _, width in CHUNKS],
        compiler_params=pltpu.CompilerParams(
            collective_id=0, has_side_effects=True, vmem_limit_bytes=VMEM_LIMIT
        ),
        cost_estimate=pl.CostEstimate(flops=60 << 30, bytes_accessed=16 << 20, transcendentals=0),
        name="fit",
    )(sources, weights, start)


def body(weights, stored_order, assignment, init_basis):
    groups, members = lax.axis_size("grp"), lax.axis_size("mem")
    experts = weights.shape[0] * members
    capacity = experts // groups + experts // (2 * groups)
    sources = slot_sources(stored_order, assignment, groups, capacity)
    basis, coefficients = fit(weights, sources, init_basis[0], groups, members, capacity)
    return (basis[None], coefficients[None])


def solution(mesh):
    return jax.shard_map(
        body,
        mesh=mesh,
        in_specs=(P("mem", None, "grp"), P(), P(), P("grp", None, None)),
        out_specs=(P("grp", "mem", None), P("grp", None, "mem", None)),
        check_vma=False,
    )
```

```python
import jax
import jax.numpy as jnp
from jax import lax
from jax.experimental import pallas as pl
from jax.experimental.pallas import tpu as pltpu
from jax.sharding import PartitionSpec as P

ITERS = 2
NS_STEPS = 6
MESH = pl.DeviceIdType.MESH
F32 = jnp.float32
BF16 = jnp.bfloat16
ROW = 16
VMEM_LIMIT = 60 * 1024 * 1024


def remote(src, dst, send, recv, device):
    return pltpu.make_async_remote_copy(
        src_ref=src, dst_ref=dst, send_sem=send, recv_sem=recv, device_id=device, device_id_type=MESH
    )


def greet(peers):
    barrier = pltpu.get_barrier_semaphore()
    for peer in peers:
        pl.semaphore_signal(barrier, inc=1, device_id=peer, device_id_type=MESH)
    pl.semaphore_wait(barrier, len(peers))


def slot_sources(stored_order, assignment, groups, capacity):
    assign = assignment[:, 0]
    experts = assign.shape[0]
    ids = jnp.arange(experts, dtype=jnp.int32)
    before = (assign[None, :] == assign[:, None]) & (ids[None, :] < ids[:, None])
    whole = jnp.where(ids[None, :] < assign[:, None], capacity, 0)
    slot = jnp.sum(whole + before.astype(jnp.int32), axis=1)
    slot_of_position = jnp.sum(jnp.where(stored_order[:, None] == ids[None, :], slot[None, :], 0), axis=1)
    slots = jnp.arange(groups * capacity, dtype=jnp.int32)
    return jnp.min(jnp.where(slot_of_position[None, :] == slots[:, None], ids[None, :], experts), axis=1)


NN = (((1,), (0,)), ((), ()))
NT = (((1,), (1,)), ((), ()))


def mm(a, b, dims=NN):
    return lax.dot_general(a, b, dims, preferred_element_type=F32)


def split(x):
    high = x.astype(BF16)
    return high, (x - high.astype(F32)).astype(BF16)


def mm3(a, b, dims=NN):
    return mm(a[0], b[0], dims) + (mm(a[0], b[1], dims) + mm(a[1], b[0], dims))


def eye(n):
    return (lax.broadcasted_iota(jnp.int32, (n, n), 0) == lax.broadcasted_iota(jnp.int32, (n, n), 1)).astype(F32)


def inverse_root(gram, frob):
    ident = eye(gram.shape[0])
    scaled = gram / frob
    gap = (0.5 * (ident - scaled)).astype(BF16)
    halves = split(scaled)
    scaled = scaled + (mm(halves[0], gap) + mm(halves[1], gap))
    root = ident + gap.astype(F32)
    for inner in range(1, NS_STEPS):
        upper, lower = split(root), split(scaled)
        gap = (0.5 * (ident - mm3(upper, lower))).astype(BF16)
        root = root + (mm(gap, upper[0]) + mm(gap, upper[1]))
        if inner < NS_STEPS - 1:
            scaled = scaled + (mm(lower[0], gap) + mm(lower[1], gap))
    return split(root)


CHUNKS = [(0, 0, 256), (0, 256, 256), (0, 512, 512), (1, 0, 512), (1, 512, 512), (2, 0, 512), (2, 512, 256), (2, 768, 256)]
AHEAD = 3
ORDER = (2, 1, 3)
LAG = 3
CUTS = 2
AORDER = (1, 3, 2)


def fit(weights, sources, start, groups, members, capacity):
    held, rows_all, columns = weights.shape
    experts = held * members
    share = rows_all // members
    parts = share // ROW
    part_rows = capacity * ROW
    total = len(CHUNKS)
    depth, rank = start.shape
    rows = parts * part_rows
    chunk = depth // 8 // CUTS
    half = rank // 2
    quarter = half // 4

    def kernel(
        sources_ref, weights_ref, start_ref, basis_ref, coef_ref,
        w_ref, b_ref, proj, proj_t, full, out1, in1, sum1, in2, sum2, in3, root_hi, root_lo, gram_ref, scale_ref,
        start_sem, own_sem, keep_sem, a_send, a_recv, b_send, b_recv, send, recv, *buffers,
    ):
        landed, packed = buffers[:total], buffers[total:]
        g, m = lax.axis_index("grp"), lax.axis_index("mem")
        x, z, c = m // 8, lax.rem(m // 2, 4), lax.rem(m, 2)
        sib = 1 - c
        member = lambda xx, zz, cc: (g, 8 * xx + 2 * zz + cc)
        turn = lambda v, o: lax.rem(v + o, 4)
        others = [(g, m ^ (k ^ (k >> 1))) for k in range(1, members)]
        across = [(lax.rem(g + k, groups), m) for k in range(1, groups)]
        load_start = pltpu.make_async_copy(start_ref, b_ref, start_sem)
        load_start.start()
        greet(others + across)

        def piece(ci, who):
            r, c0, width = CHUNKS[ci]
            return weights_ref.at[:, pl.ds(share * who + ROW * r, ROW), pl.ds(c0, width)]

        def own(ci):
            return pltpu.make_async_copy(piece(ci, m), landed[ci].at[pl.ds(held * m, held)], own_sem.at[ci])

        def launch(ci):
            own(ci).start()
            for dev in others:
                remote(
                    piece(ci, dev[1]), landed[ci].at[pl.ds(held * m, held)], a_send.at[ci], a_recv.at[ci], dev
                ).start()
            landed[ci][experts] = jnp.zeros((ROW, CHUNKS[ci][2]), BF16)

        def target(ci, source_group):
            r, c0, width = CHUNKS[ci]
            return w_ref.at[pl.ds(r * part_rows, part_rows), pl.ds(pl.multiple_of(columns * source_group + c0, 128), width)]

        def keep(ci):
            return pltpu.make_async_copy(packed[ci].at[g], target(ci, g), keep_sem.at[ci])

        def cross(ci, k):
            dev = across[k - 1]
            return remote(packed[ci].at[dev[0]], target(ci, g), b_send.at[ci, k], b_recv.at[ci, k], dev)

        for ci in range(min(AHEAD, total)):
            launch(ci)
        for ci in range(total):
            own(ci).wait()
            arrivals = landed[ci].at[pl.ds(0, experts - held)]
            pltpu.make_async_copy(arrivals, arrivals, a_recv.at[ci]).wait()

            def pack(k, carry, ci=ci):
                for group in range(groups):
                    packed[ci][group, pl.ds(pl.multiple_of(k * ROW, ROW), ROW), :] = landed[ci][
                        sources_ref[group * capacity + k]
                    ]
                return carry

            lax.fori_loop(0, capacity, pack, 0)
            for k in range(1, groups):
                cross(ci, k).start()
            keep(ci).start()
            if ci + AHEAD < total:
                launch(ci + AHEAD)

        load_start.wait()
        proj[...] = jnp.zeros_like(proj)
        ident = eye(rank).astype(BF16)
        for ci in range(total):
            keep(ci).wait()
            for k in range(1, groups):
                cross(ci, k).wait()
            r, c0, width = CHUNKS[ci]
            at = slice(r * part_rows, (r + 1) * part_rows)
            term = None
            for group in range(groups):
                cols = slice(columns * group + c0, columns * group + c0 + width)
                more = mm(w_ref[at, cols], b_ref[cols, :])
                term = more if term is None else term + more
            proj[at, :] += term
            if ci + 1 == total or CHUNKS[ci + 1][0] != r:
                proj_t[:, at] = mm(ident, proj[at, :].astype(BF16), NT).astype(BF16)

        sibling = member(x, z, sib)
        xs = [None] + [member(turn(x, o), z, c) for o in (1, 2, 3)]
        zs = [None] + [member(x, turn(z, o), c) for o in (1, 2, 3)]
        first, second = (xs, zs), (zs, xs)
        place, other = (x, z), (z, x)

        def copy(stage, h, u, o, src, dst, dev):
            return remote(src, dst, send.at[stage, h, u, o], recv.at[stage, h, u, o], dev)

        HALVES = (0, 1)
        steps = [(u, o, h) for u in range(CUTS) for o in ORDER + (0,) for h in HALVES]

        def index_of(core, q, u):
            return (core * 4 + q) * CUTS + u

        def columns_of(core, q, u):
            return pl.ds(pl.multiple_of(index_of(core, q, u) * chunk, chunk), chunk)

        def image_piece(core, q, u, h):
            left = proj_t.at[pl.ds(h * half, half)]
            cols = columns_of(core, q, u)
            cut = rows // 256 * 256
            return mm(left[:, 0:cut], w_ref[0:cut, cols]) + mm(left[:, cut:rows], w_ref[cut:rows, cols])

        def sweep(it, carry):
            ship1, ship2, ship3, ship4, ship5, ship6 = {}, {}, {}, {}, {}, {}

            def give(u, o, h):
                out1[h, u, o] = image_piece(sib, turn(place[h], o), u, h).astype(BF16)
                ship1[u, o, h] = copy(0, h, u, o, out1.at[h, u, o], in1.at[h, u, o], sibling)
                ship1[u, o, h].start()

            def take(u, o, h):
                mine = image_piece(c, turn(place[h], o), u, h)
                ship1[u, o, h].wait_recv()
                sum1[h, u, o] = (mine + in1[h, u, o].astype(F32)).astype(BF16)
                if o:
                    ship2[u, o, h] = copy(1, h, u, o, sum1.at[h, u, o], in2.at[h, u, o], first[h][o])
                    ship2[u, o, h].start()

            def sum_first(u):
                for h in HALVES:
                    for o in (1, 2, 3):
                        ship2[u, o, h].wait_recv()
                    sum2[h, u] = (
                        (sum1[h, u, 0].astype(F32) + in2[h, u, 1].astype(F32))
                        + (in2[h, u, 2].astype(F32) + in2[h, u, 3].astype(F32))
                    ).astype(BF16)
                    for o in ORDER:
                        rows_there = pl.ds(pl.multiple_of(turn(other[h], o) * quarter, quarter), quarter)
                        ship3[u, o, h] = copy(2, h, u, o, sum2.at[h, u, rows_there], in3.at[h, u, o], second[h][o])
                        ship3[u, o, h].start()

            def sum_second(u):
                for h in HALVES:
                    for o in (1, 2, 3):
                        ship3[u, o, h].wait_recv()
                    mine_rows = pl.ds(pl.multiple_of(other[h] * quarter, quarter), quarter)
                    here = pl.ds(pl.multiple_of(h * half + other[h] * quarter, quarter), quarter)
                    total = (sum2[h, u, mine_rows].astype(F32) + in3[h, u, 1].astype(F32)) + (
                        in3[h, u, 2].astype(F32) + in3[h, u, 3].astype(F32)
                    )
                    at = index_of(c, place[h], u)
                    full[at, here, :] = total.astype(BF16)
                    for o in ORDER:
                        spot = full.at[at, here]
                        ship4[u, o, h] = copy(3, h, u, o, spot, spot, second[h][o])
                        ship4[u, o, h].start()

            def origin(o, h):
                return turn(place[h], (4 - o) % 4)

            def hand_over(u, o, h):
                spot = full.at[index_of(c, origin(o, h), u), pl.ds(h * half, half)]
                ship6[u, o, h] = copy(5, h, u, o, spot, spot, sibling)
                ship6[u, o, h].start()

            def spread(u):
                for h in HALVES:
                    for o in (1, 2, 3):
                        ship4[u, o, h].wait_recv()
                    spot = full.at[index_of(c, place[h], u), pl.ds(h * half, half)]
                    hand_over(u, 0, h)
                    for o in ORDER:
                        ship5[u, o, h] = copy(4, h, u, o, spot, spot, first[h][o])
                        ship5[u, o, h].start()

            def collect(u, o):
                for h in HALVES:
                    ship5[u, o, h].wait_recv()
                    hand_over(u, o, h)

            def absorb(u, o, start=False):
                for h in HALVES:
                    ship6[u, o, h].wait_recv()
                    cols = slice(h * half, (h + 1) * half)
                    q = origin(o, h)
                    blocks = [full[index_of(core, q, u), h * half : (h + 1) * half, :] for core in (c, sib)]
                    square = mm(blocks[0], blocks[0], NT) + mm(blocks[1], blocks[1], NT)
                    if start:
                        gram_ref[h] = square
                    else:
                        gram_ref[h] += square
                    for r in range(0, rows, part_rows):
                        at = slice(r, r + part_rows)
                        term = mm(w_ref[at, columns_of(c, q, u)], blocks[0], NT) + mm(
                            w_ref[at, columns_of(sib, q, u)], blocks[1], NT
                        )
                        if start:
                            proj[at, cols] = term
                        else:
                            proj[at, cols] += term

            for i in range(len(steps) + LAG):
                if i < len(steps):
                    give(*steps[i])
                if i >= LAG:
                    take(*steps[i - LAG])
            sum_first(0)
            for u in range(CUTS):
                sum_second(u)
                if u + 1 < CUTS:
                    sum_first(u + 1)
                spread(u)
            for step in steps:
                ship1[step].wait_send()
                if step[1]:
                    for ship in (ship2, ship3):
                        ship[step].wait_send()
            waiting = []
            for u in range(CUTS):
                waiting.append((u, 0))
            absorb(0, 0, True)
            waiting = waiting[1:]
            for u in range(CUTS):
                for o in AORDER:
                    collect(u, o)
                    waiting.append((u, o))
                    absorb(*waiting.pop(0))
            for item in waiting:
                absorb(*item)

            cross_gram = None
            for d in range(8 * CUTS):
                term = mm(full[d, 0:half, :], full[d, half:rank, :], NT)
                cross_gram = term if cross_gram is None else cross_gram + term
            gram = jnp.concatenate(
                [
                    jnp.concatenate([gram_ref[0], cross_gram], axis=1),
                    jnp.concatenate([cross_gram.T, gram_ref[1]], axis=1),
                ],
                axis=0,
            )
            frob = jnp.sqrt(jnp.sum(gram * gram)) + 1e-06
            root = inverse_root(gram, frob)
            scale = jnp.sqrt(jnp.float32(depth) / frob)
            root_hi[...] = root[0]
            root_lo[...] = root[1]
            scale_ref[0] = scale

            @pl.when(it + 1 < ITERS)
            def _():
                proj_t[...] = (mm3(root, split(proj[...]), NT) * scale).astype(BF16)

            for step in steps:
                ship6[step].wait_send()
                if step[1]:
                    for ship in (ship4, ship5):
                        ship[step].wait_send()
            return carry

        lax.fori_loop(0, ITERS, sweep, 0)

        root = (root_hi[...], root_lo[...])
        scale = scale_ref[0]
        for r in range(parts):
            value = mm3(split(proj[r * part_rows : (r + 1) * part_rows, :]), root) * scale
            coef_ref[:, r * ROW : (r + 1) * ROW, :] = value.astype(BF16).reshape(capacity, ROW, rank)
        per = chunk // 128
        block = full[m // per, :, pl.ds(pl.multiple_of(lax.rem(m, per) * 128, 128), 128)]
        turned = mm(eye(128).astype(BF16), block, NT).astype(BF16)
        basis_ref[...] = ((mm(turned, root[0]) + mm(turned, root[1])) * scale).astype(BF16)
        for ci in range(total):
            sent = landed[ci].at[pl.ds(0, experts - held)]
            pltpu.make_async_copy(sent, sent, a_send.at[ci]).wait()

    return pl.pallas_call(
        kernel,
        out_shape=(
            jax.ShapeDtypeStruct((128, rank), BF16),
            jax.ShapeDtypeStruct((capacity, parts * ROW, rank), BF16),
        ),
        in_specs=[pl.BlockSpec(memory_space=pltpu.SMEM)] + [pl.BlockSpec(memory_space=pl.ANY)] * 2,
        out_specs=(pl.BlockSpec(memory_space=pltpu.VMEM),) * 2,
        scratch_shapes=[
            pltpu.VMEM((rows, depth), BF16),
            pltpu.VMEM((depth, rank), BF16),
            pltpu.VMEM((rows, rank), F32),
            pltpu.VMEM((rank, rows), BF16),
            pltpu.VMEM((8 * CUTS, rank, chunk), BF16),
            pltpu.VMEM((2, CUTS, 4, half, chunk), BF16),
            pltpu.VMEM((2, CUTS, 4, half, chunk), BF16),
            pltpu.VMEM((2, CUTS, 4, half, chunk), BF16),
            pltpu.VMEM((2, CUTS, 4, half, chunk), BF16),
            pltpu.VMEM((2, CUTS, half, chunk), BF16),
            pltpu.VMEM((2, CUTS, 4, quarter, chunk), BF16),
            pltpu.VMEM((rank, rank), BF16),
            pltpu.VMEM((rank, rank), BF16),
            pltpu.VMEM((2, half, half), F32),
            pltpu.SMEM((1,), F32),
            pltpu.SemaphoreType.DMA,
            pltpu.SemaphoreType.DMA((total,)),
            pltpu.SemaphoreType.DMA((total,)),
            pltpu.SemaphoreType.DMA((total,)),
            pltpu.SemaphoreType.DMA((total,)),
            pltpu.SemaphoreType.DMA((total, groups)),
            pltpu.SemaphoreType.DMA((total, groups)),
            pltpu.SemaphoreType.DMA((6, 2, CUTS, 4)),
            pltpu.SemaphoreType.DMA((6, 2, CUTS, 4)),
        ]
        + [pltpu.VMEM((experts + 1, ROW, width), BF16) for _, _, width in CHUNKS]
        + [pltpu.VMEM((groups, part_rows, width), BF16) for _, _, width in CHUNKS],
        compiler_params=pltpu.CompilerParams(
            collective_id=0, has_side_effects=True, vmem_limit_bytes=VMEM_LIMIT
        ),
        cost_estimate=pl.CostEstimate(flops=60 << 30, bytes_accessed=16 << 20, transcendentals=0),
        name="fit",
    )(sources, weights, start)


def body(weights, stored_order, assignment, init_basis):
    groups, members = lax.axis_size("grp"), lax.axis_size("mem")
    experts = weights.shape[0] * members
    capacity = experts // groups + experts // (2 * groups)
    sources = slot_sources(stored_order, assignment, groups, capacity)
    basis, coefficients = fit(weights, sources, init_basis[0], groups, members, capacity)
    return (basis[None], coefficients[None])


def solution(mesh):
    return jax.shard_map(
        body,
        mesh=mesh,
        in_specs=(P("mem", None, "grp"), P(), P(), P("grp", None, None)),
        out_specs=(P("grp", "mem", None), P("grp", None, "mem", None)),
        check_vma=False,
    )
```
